32 devices in a mesh: fsdp: 2 (over y), dp: 4 (over z), tensor: 4 (over x, core).
Axes of the slice: x: 2, y: 2, z: 4, core: 2. Of those that a mesh axis runs over, the one named last changes fastest.
Arguments:
- master_weight: float32 [4096, 14336], P(('fsdp', 'dp'), 'tensor'), may hold values from -0.09375 to 0.09375
- first_moment: bfloat16 [4096, 14336], P(('fsdp', 'dp'), 'tensor'), may hold values from -6 to 6
- second_moment: bfloat16 [4096, 14336], P(('fsdp', 'dp'), 'tensor'), may hold values from 0.25 to 16
- teacher_weight: float32 [4096, 14336], P(('fsdp', 'dp'), 'tensor'), may hold values from -0.09375 to 0.09375
- grad_parts: bfloat16 [4, 4096, 14336], P('dp', 'fsdp', 'tensor'), may hold values from -6 to 6
- embed_table: bfloat16 [4096, 64128], P(('fsdp', 'dp', 'tensor')), may hold values from -6 to 6
- token_ids: int32 [2, 256], P('fsdp'), may hold values from 0 to 64127
- pair_ids: int32 [2, 256], P('fsdp'), may hold values from 0 to 7, never falling along the last dimension, each value on 1 to 64 neighbouring positions
- class_head: bfloat16 [4, 3584, 256], P('tensor', 'dp'), may hold values from -0.046875 to 0.046875
Outputs:
- master_new: float32 [4096, 14336], P(('fsdp', 'dp'), 'tensor')
- first_new: bfloat16 [4096, 14336], P(('fsdp', 'dp'), 'tensor')
- second_new: bfloat16 [4096, 14336], P(('fsdp', 'dp'), 'tensor')
- teacher_new: float32 [4096, 14336], P(('fsdp', 'dp'), 'tensor')
- class_logits: float32 [2, 8, 256], P('fsdp')
The draws below stay inside these ranges and needn't reach their ends.
Inputs may be any that keep to these rules, and one draw needn't show every extreme that they name: `pair_ids`: in every row the pair numbers never fall, and each of the 8 pairs holds 1 to 64 tokens, one of them exactly 64.
All inputs are finite; a program needn't handle non-finite values.
Results may differ from the reference program's by a relative error of at most 0.0055.
Values may be sent and summed in bfloat16 or wider, within the bound.
A program may use at most 192 MiB of HBM per device.

```python
import math
import jax
import jax.numpy as jnp
import numpy as np
from jax import lax

D = 4096
FF = 14336
VOCAB = 64128
CLASSES = 256
PAIRS = 8
TOK_GRP = 256
MOST = 64
FF_T = 3584
N_FSDP = 2
N_DP = 4
N_TENSOR = 4


def draw_embed_table(key, part):
    key_rows, key_cols, key_base = jax.random.split(key, 3)
    row_scale = jnp.exp(jax.random.uniform(key_rows, (D, 1), jnp.float32, 0.0, 2.5))
    col_scale = jnp.exp(jax.random.uniform(key_cols, (1, VOCAB), jnp.float32, 0.0, 2.5))
    base = jax.random.truncated_normal(key_base, -4.0, 4.0, (D, VOCAB), jnp.float32)
    return (0.01 * row_scale * col_scale * base).astype(jnp.bfloat16)


def touch_ends(result, rng, low, largest):
    place = [jax.random.randint(jax.random.fold_in(rng, axis), (), 0, length) for axis, length in enumerate(result.shape)]
    widest = result.shape.index(max(result.shape))
    neighbour = place[:widest] + [(place[widest] + 1) % result.shape[widest]] + place[widest + 1:]
    return result.at[tuple(place)].set(low).at[tuple(neighbour)].set(largest)


def strengthened(drawn, rng, source, target, parts, factor):
    owner, partner = [(jnp.arange(drawn.shape[axis_at]) // (drawn.shape[axis_at] // parts)).reshape([-1 if axis == axis_at else 1 for axis in range(drawn.ndim)]) for axis_at in (source, target)]
    chosen = jax.random.permutation(rng, parts)[partner]
    strong = (owner == chosen) | (owner == (partner + parts // 2) % parts)
    return jnp.where(strong, factor * drawn, drawn)


def block_levels(rng, shape, cuts, smallest, top_value):
    def one(dim, parts):
        steps = jax.random.uniform(jax.random.fold_in(jax.random.fold_in(rng, 6), dim), (parts,), jnp.float32, smallest / len(cuts), top_value / len(cuts))
        return jnp.repeat(jnp.exp(steps), shape[dim] // parts).reshape((-1,) + (1,) * (len(shape) - dim - 1))

    level = one(*cuts[0])
    for cut in cuts[1:]:
        level = level * one(*cut)
    return level


def rank_table(amount, skew):
    weights = [(1 << 20) // math.isqrt(grade ** skew) + 1 for grade in range(1, amount + 1)]
    scale = 1 + sum(weights) // (1 << 30)
    return np.cumsum(np.array([max(1, weight // scale) for weight in weights]))


def ranked_ids(rng, dims, count, slope):
    listing = rank_table(count, slope)
    ticket = jax.random.randint(jax.random.fold_in(rng, 1), dims, 0, int(listing[count - 1]))
    standing = jnp.searchsorted(jnp.asarray(listing, jnp.int32), ticket, side="right")
    return jax.random.permutation(jax.random.fold_in(rng, 2), count)[standing].astype(jnp.int32)


def profile(number_of, total, limit, skew):
    weights = [(1 << 20) // math.isqrt(grade ** skew) + 1 for grade in range(2, number_of + 1)]
    surplus, counts = total - limit - (number_of - 1), [1] * (number_of - 1)
    while surplus > 0:
        free = [i for i in range(number_of - 1) if counts[i] < limit]
        pool, left = sum([weights[i] for i in free]), surplus
        for i in free:
            addition = min(limit - counts[i], max(1, left * weights[i] // pool), surplus)
            counts[i] = counts[i] + addition
            surplus = surplus - addition
    return np.array([limit] + counts)


def uneven_parts(stream_key, number_of, total, most, skew):
    if number_of == 2:
        one = jax.random.randint(stream_key, (), max(1, total - most), min(most, total - 1) + 1)
        return jnp.stack([one, total - one])
    tallies = jnp.asarray(profile(number_of, total, most, skew), jnp.int32)
    twos = (number_of - 1) // 2
    donor, receiver = tallies[1:1 + 2 * twos:2], tallies[2:2 + 2 * twos:2]
    slack = jnp.minimum(donor - 1, most - receiver)
    moved = jax.random.randint(jax.random.fold_in(stream_key, 1), (twos,), 0, 1 << 20) % (slack + 1)
    tallies = tallies.at[1:1 + 2 * twos:2].set(donor - moved).at[2:2 + 2 * twos:2].set(receiver + moved)
    return tallies[jax.random.permutation(jax.random.fold_in(stream_key, 2), number_of)]


def centred(stream_key, extent, deviation, most, cuts=(), kind=jnp.bfloat16):
    result = jax.random.normal(stream_key, extent, jnp.float32) * deviation
    if len(cuts) > 0:
        result = block_levels(stream_key, extent, cuts, -0.22, 0.18) * result
    return jnp.clip(result, min=-most, max=most).astype(kind)


def gaussian_with(rng, dims, scale, reach, cuts, heavy, kind=jnp.bfloat16):
    result = scale * jax.random.normal(rng, dims, jnp.float32)
    if cuts:
        result = result * block_levels(rng, dims, cuts, -0.22, 0.18)
    return jnp.clip(strengthened(result, jax.random.fold_in(rng, 3), *heavy), -reach, reach).astype(kind)


def setup_inputs(seed: int = 0) -> dict:
    key_of = jax.random.split(jax.random.key(seed), 10)
    master_weight = centred(key_of[0], (D, FF), D ** -0.5, 0.09375, ((0, 8), (1, 4)), jnp.float32)
    first_moment = centred(key_of[1], (D, FF), 1.0, 6.0, ((0, 8), (1, 4)))
    second_moment = jnp.clip(jnp.exp(math.log(16.0) - 4.158883 * jax.random.uniform(key_of[2], (D, FF), jnp.float32) ** block_levels(key_of[2], (D, FF), ((0, 8), (1, 4)), -0.2, 0.2)), 0.25, 16.0).astype(jnp.bfloat16)
    teacher_weight = centred(key_of[3], (D, FF), D ** -0.5, 0.09375, ((0, 8), (1, 4)), jnp.float32)
    grad_parts = gaussian_with(key_of[4], (N_DP, D, FF), 1.0, 6.0, ((0, 4), (1, 2), (2, 4)), (0, 1, 4, 2.0))
    embed_table = draw_embed_table(jax.random.fold_in(key_of[9], 71), 0)
    token_ids = touch_ends(ranked_ids(key_of[6], (N_FSDP, TOK_GRP), VOCAB, 2), jax.random.fold_in(key_of[6], 3), 0, VOCAB - 1).astype(jnp.int32)
    pair_ids = jax.vmap(lambda own: jnp.searchsorted(jnp.cumsum(uneven_parts(own, PAIRS, TOK_GRP, MOST, 1)), jnp.arange(TOK_GRP), side="right"))(jax.random.split(key_of[7], N_FSDP)).reshape((N_FSDP, TOK_GRP)).astype(jnp.int32)
    class_head = centred(key_of[8], (N_TENSOR, FF_T, CLASSES), FF ** -0.5, 0.046875, ((0, 4), (1, 4)))
    return {"master_weight": master_weight, "first_moment": first_moment, "second_moment": second_moment, "teacher_weight": teacher_weight, "grad_parts": grad_parts, "embed_table": embed_table, "token_ids": token_ids, "pair_ids": pair_ids, "class_head": class_head}


beta_one = 0.9
beta_two = 0.95
learn_rate = 0.001
decay_rate = 0.1
ema_keep = 0.99

def reference(master_weight, first_moment, second_moment, teacher_weight, grad_parts, embed_table, token_ids, pair_ids, class_head):
    gradient = grad_parts[0].astype(jnp.float32)
    for member in range(1, N_DP):
        gradient = gradient + grad_parts[member].astype(jnp.float32)
    first_full = beta_one * first_moment.astype(jnp.float32) + (1.0 - beta_one) * gradient
    second_full = beta_two * second_moment.astype(jnp.float32) + (1.0 - beta_two) * gradient * gradient
    master_new = master_weight - learn_rate * (first_full / (jnp.sqrt(second_full) + 1e-08) + decay_rate * master_weight)
    teacher_new = ema_keep * teacher_weight + (1.0 - ema_keep) * master_new
    teacher_half = teacher_new.astype(jnp.bfloat16)
    head_rows = class_head.reshape(FF, CLASSES)

    def label_group(inputs):
        group_ids, group_pairs = inputs
        picked = jnp.take(embed_table, group_ids, axis=1).astype(jnp.float32)
        scale = lax.rsqrt(lax.optimization_barrier(jnp.mean(picked * picked, axis=0, keepdims=True)) + 1e-05)
        normed = (picked * scale).astype(jnp.bfloat16)
        hidden = jnp.dot(normed.T, teacher_half, preferred_element_type=jnp.float32)
        active = jax.nn.silu(hidden)
        member_of = (group_pairs[None, :] == jnp.arange(PAIRS, dtype=jnp.int32)[:, None]).astype(jnp.float32)
        totals = jnp.dot(member_of, active, precision=lax.Precision.HIGHEST)
        pooled = (totals / lax.optimization_barrier(jnp.sum(member_of, axis=1, keepdims=True))).astype(jnp.bfloat16)
        return jnp.dot(pooled, head_rows, preferred_element_type=jnp.float32)
    class_logits = lax.map(label_group, (token_ids, pair_ids))
    return (master_new, first_full.astype(jnp.bfloat16), second_full.astype(jnp.bfloat16), teacher_new, class_logits)
```

```python
import jax
import jax.numpy as jnp
from jax import lax
from jax.sharding import PartitionSpec as P

PAIRS = 8


beta_one = 0.9
beta_two = 0.95
learn_rate = 0.001
decay_rate = 0.1
ema_keep = 0.99


def spread(block, axes):
    count = lax.axis_size(axes)
    copies = jnp.broadcast_to(block[None], (count,) + block.shape)
    return lax.all_to_all(copies, axes, split_axis=0, concat_axis=0, tiled=True)


def update(master_weight, first_moment, second_moment, teacher_weight, gradient):
    gradient = gradient.astype(jnp.float32)
    first_full = beta_one * first_moment.astype(jnp.float32) + (1.0 - beta_one) * gradient
    second_full = (
        beta_two * second_moment.astype(jnp.float32) + (1.0 - beta_two) * gradient * gradient
    )
    master_new = master_weight - learn_rate * (
        first_full / (jnp.sqrt(second_full) + 1e-08) + decay_rate * master_weight
    )
    teacher_new = ema_keep * teacher_weight + (1.0 - ema_keep) * master_new
    return (
        master_new,
        first_full.astype(jnp.bfloat16),
        second_full.astype(jnp.bfloat16),
        teacher_new,
    )


def own_features(embed_table, token_ids):
    every_id = spread(token_ids, "fsdp").reshape(-1)
    picked = jnp.take(embed_table, every_id, axis=1)
    rows = spread(picked, "tensor").reshape(-1, every_id.shape[0])
    values = rows.astype(jnp.float32)
    squares = spread(jnp.sum(values * values, axis=0), ("fsdp", "dp"))
    features = rows.shape[0] * squares.shape[0]
    scale = lax.rsqrt(jnp.sum(squares, axis=0, keepdims=True) / features + 1e-05)
    return (values * scale).astype(jnp.bfloat16)


def shards(
    master_weight,
    first_moment,
    second_moment,
    teacher_weight,
    grad_parts,
    embed_table,
    token_ids,
    pair_ids,
    class_head,
):
    replicas = lax.axis_size("dp")
    groups = lax.axis_size("fsdp")
    tokens = token_ids.shape[1]
    width = master_weight.shape[1] // replicas
    head_part = class_head[0]
    partial = grad_parts[0]

    steps = [256] * (width // 256) + ([width % 256] if width % 256 else [])
    bounds = [(sum(steps[:i]), sum(steps[: i + 1])) for i in range(len(steps))]

    def columns(whole, low, high):
        return [whole[:, d * width + low : d * width + high] for d in range(replicas)]

    pieces = [
        lax.psum_scatter(
            jnp.concatenate(columns(partial, low, high), axis=1),
            "dp",
            scatter_dimension=0,
            tiled=True,
        )
        for low, high in bounds
    ]

    normed = own_features(embed_table, token_ids)
    member_of = (
        pair_ids[0][None, :] == jnp.arange(PAIRS, dtype=jnp.int32)[:, None]
    ).astype(jnp.float32)
    sizes = jnp.sum(member_of, axis=1, keepdims=True)

    terms = jnp.zeros((PAIRS, head_part.shape[1]), jnp.float32)
    for (low, high), piece in zip(bounds, pieces):
        step = high - low
        halves = [
            update(*own)[3].astype(jnp.bfloat16)
            for own in zip(
                columns(master_weight, low, high),
                columns(first_moment, low, high),
                columns(second_moment, low, high),
                columns(teacher_weight, low, high),
                [piece[:, d * step : (d + 1) * step] for d in range(replicas)],
            )
        ]
        teacher_half = jnp.stack(halves)
        sent = jnp.einsum(
            "fk,dfw->dkw", normed, teacher_half, preferred_element_type=jnp.float32
        ).astype(jnp.bfloat16)
        sent = sent.reshape(replicas * groups, tokens, step)
        received = lax.all_to_all(
            sent, ("dp", "fsdp"), split_axis=0, concat_axis=0, tiled=True
        )
        hidden = jnp.sum(received.astype(jnp.float32), axis=0)
        active = jax.nn.silu(hidden)
        totals = jnp.dot(member_of, active, precision=lax.Precision.HIGHEST)
        pooled = (totals / sizes).astype(jnp.bfloat16)
        terms = terms + jnp.dot(
            pooled, head_part[low:high], preferred_element_type=jnp.float32
        )

    gradient = jnp.concatenate(
        [
            piece[:, d * (high - low) : (d + 1) * (high - low)]
            for d in range(replicas)
            for (low, high), piece in zip(bounds, pieces)
        ],
        axis=1,
    )
    updated = update(master_weight, first_moment, second_moment, teacher_weight, gradient)
    logits = jnp.sum(spread(terms, ("dp", "tensor")), axis=0)[None]
    return (*updated, logits)


def solution(mesh):
    placed = (
        P(("fsdp", "dp"), "tensor"),
        P(("fsdp", "dp"), "tensor"),
        P(("fsdp", "dp"), "tensor"),
        P(("fsdp", "dp"), "tensor"),
        P("dp", "fsdp", "tensor"),
        P(("fsdp", "dp", "tensor"), None),
        P("fsdp", None),
        P("fsdp", None),
        P("tensor", "dp", None),
    )
    return jax.shard_map(
        shards,
        mesh=mesh,
        in_specs=placed,
        out_specs=(
            P(("fsdp", "dp"), "tensor"),
            P(("fsdp", "dp"), "tensor"),
            P(("fsdp", "dp"), "tensor"),
            P(("fsdp", "dp"), "tensor"),
            P("fsdp", None, None),
        ),
        check_vma=False,
    )
```

```python
import jax
import jax.numpy as jnp
from jax import lax
from jax.experimental.layout import Layout, with_layout_constraint
from jax.sharding import PartitionSpec as P

PAIRS = 8


beta_one = 0.9
beta_two = 0.95
learn_rate = 0.001
decay_rate = 0.1
ema_keep = 0.99


def row_major(block):
    return with_layout_constraint(block, Layout(major_to_minor=tuple(range(block.ndim))))


def spread(block, axes):
    count = lax.axis_size(axes)
    copies = jnp.broadcast_to(block[None], (count,) + block.shape)
    return lax.all_to_all(copies, axes, split_axis=0, concat_axis=0, tiled=True)


def update(master_weight, first_moment, second_moment, teacher_weight, gradient):
    gradient = gradient.astype(jnp.float32)
    first_full = beta_one * first_moment.astype(jnp.float32) + (1.0 - beta_one) * gradient
    second_full = (
        beta_two * second_moment.astype(jnp.float32) + (1.0 - beta_two) * gradient * gradient
    )
    master_new = master_weight - learn_rate * (
        first_full / (jnp.sqrt(second_full) + 1e-08) + decay_rate * master_weight
    )
    teacher_new = ema_keep * teacher_weight + (1.0 - ema_keep) * master_new
    return (
        master_new,
        first_full.astype(jnp.bfloat16),
        second_full.astype(jnp.bfloat16),
        teacher_new,
    )


def own_features(embed_table, token_ids):
    every_id = spread(token_ids, "fsdp").reshape(-1)
    picked = jnp.take(embed_table, every_id, axis=1)
    rows = spread(picked, "tensor").reshape(-1, every_id.shape[0])
    values = rows.astype(jnp.float32)
    squares = spread(jnp.sum(values * values, axis=0), ("fsdp", "dp"))
    features = rows.shape[0] * squares.shape[0]
    scale = lax.rsqrt(jnp.sum(squares, axis=0, keepdims=True) / features + 1e-05)
    return (values * scale).astype(jnp.bfloat16)


def shards(
    master_weight,
    first_moment,
    second_moment,
    teacher_weight,
    grad_parts,
    embed_table,
    token_ids,
    pair_ids,
    class_head,
):
    replicas = lax.axis_size("dp")
    groups = lax.axis_size("fsdp")
    tokens = token_ids.shape[1]
    width = master_weight.shape[1] // replicas
    head_part = class_head[0]
    partial = grad_parts[0]

    steps = [256] * (width // 256) + ([width % 256] if width % 256 else [])
    bounds = [(sum(steps[:i]), sum(steps[: i + 1])) for i in range(len(steps))]

    def columns(whole, low, high):
        return [whole[:, d * width + low : d * width + high] for d in range(replicas)]

    pieces = [
        row_major(
            lax.psum_scatter(
                row_major(jnp.concatenate(columns(partial, low, high), axis=1)),
                "dp",
                scatter_dimension=0,
                tiled=True,
            )
        )
        for low, high in bounds
    ]

    normed = own_features(embed_table, token_ids)
    turned = row_major(normed.T)
    member_of = (
        pair_ids[0][None, :] == jnp.arange(PAIRS, dtype=jnp.int32)[:, None]
    ).astype(jnp.float32)
    sizes = jnp.sum(member_of, axis=1, keepdims=True)

    terms = jnp.zeros((PAIRS, head_part.shape[1]), jnp.float32)
    for at, (low, high) in enumerate(bounds):
        step = high - low
        if at:
            terms, pieces[at] = lax.optimization_barrier((terms, pieces[at]))
        piece = pieces[at]
        halves = [
            row_major(update(*own)[3].astype(jnp.bfloat16))
            for own in zip(
                columns(master_weight, low, high),
                columns(first_moment, low, high),
                columns(second_moment, low, high),
                columns(teacher_weight, low, high),
                [piece[:, d * step : (d + 1) * step] for d in range(replicas)],
            )
        ]
        sent = jnp.concatenate(
            [
                lax.dot_general(
                    turned,
                    half,
                    (((1,), (0,)), ((), ())),
                    preferred_element_type=jnp.float32,
                ).astype(jnp.bfloat16)
                for half in halves
            ],
            axis=0,
        )
        sent = row_major(sent.reshape(replicas * groups, tokens, step))
        received = lax.all_to_all(
            sent, ("dp", "fsdp"), split_axis=0, concat_axis=0, tiled=True
        )
        hidden = jnp.sum(received.astype(jnp.float32), axis=0)
        active = jax.nn.silu(hidden)
        totals = jnp.dot(member_of, active, precision=lax.Precision.HIGHEST)
        pooled = (totals / sizes).astype(jnp.bfloat16)
        terms = terms + jnp.dot(
            pooled, head_part[low:high], preferred_element_type=jnp.float32
        )

    gradient = jnp.concatenate(
        [
            piece[:, d * (high - low) : (d + 1) * (high - low)]
            for d in range(replicas)
            for (low, high), piece in zip(bounds, pieces)
        ],
        axis=1,
    )
    updated = update(master_weight, first_moment, second_moment, teacher_weight, gradient)
    logits = jnp.sum(spread(terms, ("dp", "tensor")), axis=0)[None]
    return (*updated, logits)


def solution(mesh):
    placed = (
        P(("fsdp", "dp"), "tensor"),
        P(("fsdp", "dp"), "tensor"),
        P(("fsdp", "dp"), "tensor"),
        P(("fsdp", "dp"), "tensor"),
        P("dp", "fsdp", "tensor"),
        P(("fsdp", "dp", "tensor"), None),
        P("fsdp", None),
        P("fsdp", None),
        P("tensor", "dp", None),
    )
    return jax.shard_map(
        shards,
        mesh=mesh,
        in_specs=placed,
        out_specs=(
            P(("fsdp", "dp"), "tensor"),
            P(("fsdp", "dp"), "tensor"),
            P(("fsdp", "dp"), "tensor"),
            P(("fsdp", "dp"), "tensor"),
            P("fsdp", None, None),
        ),
        check_vma=False,
    )
```
